32 devices in a mesh: segment: 4 (over y, core), seq: 8 (over z, x).
Axes of the slice: x: 2, y: 2, z: 4, core: 2. Of those that a mesh axis runs over, the one named last changes fastest.
Arguments:
- residual: bfloat16 [4, 1024, 8192], P('segment', 'seq'), may hold values from -6 to 6
- query_rows: bfloat16 [4, 2, 1024, 8192], P('segment', None, 'seq'), may hold values from -8 to 8
- key_rows: bfloat16 [4, 2, 1024, 1024], P('segment', None, 'seq'), may hold values from -6 to 6
- value_rows: bfloat16 [4, 2, 1024, 1024], P('segment', None, 'seq'), may hold values from -8 to 8
- pattern: int32 [4, 2, 8, 8, 8], P('segment'), may hold values from -1 to 7, as said below
Outputs:
- section_out: float32 [4, 1024, 8192], P('segment', 'seq')
The draws below stay inside these ranges and needn't reach their ends.
Inputs may be any that keep to these rules, and one draw needn't show every extreme that they name: `pattern`: in each row (section, layer, key-value head, query block i) slot 0 holds i; the entries that are not -1 are distinct and at most i; for every section, layer and key-value head some row has all 8 slots filled.
All inputs are finite; a program needn't handle non-finite values.
Results may differ from the reference program's by a relative error of at most 0.0035.
Values may be sent and summed in bfloat16 or wider, within the bound.
No kernel may reach another device: no remote copies, remote signals or barrier semaphores. Data moves between devices by JAX's collectives and lax.ppermute only.
A program may use at most 128 MiB of HBM per device.

```python
import math
import jax
import jax.numpy as jnp
from jax import lax

HQ = 64
HK = 8
HD = 128
LAYERS = 2
BLOCK = 128
NSEL = 8
D = 8192
TOKENS = 1024
NQB = 8
SEGMENTS = 4


def shared_draw(key):
    base_key = jax.random.fold_in(key, 11)
    key_query, key_keys = jax.random.split(base_key, 2)
    query_shape = (SEGMENTS, LAYERS, TOKENS, HQ * HD)
    key_shape = (SEGMENTS, LAYERS, TOKENS, HK * HD)
    query_vals = jnp.clip(jax.random.normal(key_query, query_shape, jnp.float32), -6.0, 6.0)
    key_vals = jnp.clip(jax.random.normal(key_keys, key_shape, jnp.float32), -6.0, 6.0)
    return (query_vals, key_vals)


def draw_query_rows(key, part):
    return shared_draw(key)[0].astype(jnp.bfloat16)


def draw_key_rows(key, part):
    return shared_draw(key)[1].astype(jnp.bfloat16)


def draw_pattern(key, part):
    extra = NSEL - 3
    row_shape = (SEGMENTS, LAYERS, HK, NQB)
    blocks = jnp.arange(NQB, dtype=jnp.int32)
    query_block = blocks.reshape(1, 1, 1, NQB)
    previous_slot = jnp.where(query_block >= 1, query_block - 1, -1)
    global_slot = jnp.where(query_block >= 2, 0, -1)
    key_score, key_cap, key_count = jax.random.split(key, 3)
    candidate = blocks.reshape(1, 1, 1, 1, NQB)
    raw_bits = jax.random.randint(key_score, row_shape + (NQB,), 0, 1 << 20)
    cand_scores = raw_bits * NQB + candidate
    usable = (candidate >= 1) & (candidate <= query_block[..., None] - 2)
    cand_scores = jnp.where(usable, cand_scores, -1)
    top_scores, picked = lax.top_k(cand_scores, extra)
    ceiling = jax.random.randint(key_cap, (SEGMENTS, LAYERS, HK, 1), 0, extra + 1)
    counts = jax.random.randint(key_count, row_shape, 0, ceiling + 1)
    counts = jnp.where(query_block == NQB - 1, extra, counts)
    slot_rank = jnp.arange(extra, dtype=jnp.int32)
    is_live = (slot_rank < counts[..., None]) & (top_scores >= 0)
    randoms = jnp.where(is_live, picked.astype(jnp.int32), -1)
    own_slot = jnp.broadcast_to(query_block, row_shape)[..., None]
    prev_col = jnp.broadcast_to(previous_slot, row_shape)[..., None]
    glob_col = jnp.broadcast_to(global_slot, row_shape)[..., None]
    return jnp.concatenate([own_slot, prev_col, glob_col, randoms], axis=-1).astype(jnp.int32)


def block_scale(own_key, shape, shards, least, high):
    gain = 1.0
    for axis_at, parts in shards:
        heights = jax.random.uniform(jax.random.fold_in(jax.random.fold_in(own_key, 6), axis_at), (parts,), jnp.float32, least / len(shards), high / len(shards))
        gain = gain * jnp.repeat(jnp.exp(heights), shape[axis_at] // parts).reshape((-1,) + (1,) * (len(shape) - 1 - axis_at))
    return gain


def gaussian(key, shape, width, limit, shards=(), kind=jnp.bfloat16):
    gain = block_scale(key, shape, shards, -0.22, 0.18) if shards else 1.0
    values = jax.random.normal(key, shape, jnp.float32) * width * gain
    return jnp.minimum(jnp.maximum(values, -limit), limit).astype(kind)


def setup_inputs(seed: int = 0) -> dict:
    key_of = jax.random.split(jax.random.key(seed), 6)
    return {
        "residual": gaussian(key_of[0], (SEGMENTS, TOKENS, D), 1.0, 6.0, ((0, 4), (1, 8))),
        "query_rows": draw_query_rows(jax.random.fold_in(key_of[5], 71), 0),
        "key_rows": draw_key_rows(jax.random.fold_in(key_of[5], 71), 0),
        "value_rows": gaussian(key_of[3], (SEGMENTS, LAYERS, TOKENS, HK * HD), 2.0, 8.0, ((0, 4), (2, 8))),
        "pattern": draw_pattern(jax.random.fold_in(key_of[5], 71), 0),
    }


def attend(q_rows, k_rows, v_rows, pattern_rows):
    token_count, head_count, head_dim = q_rows.shape
    block_count = token_count // BLOCK
    key_blocks = k_rows.reshape(block_count, BLOCK, head_dim)
    value_blocks = v_rows.reshape(block_count, BLOCK, head_dim)
    query_blocks = q_rows.reshape(block_count // 4, 4, BLOCK, head_count, head_dim)
    chosen_blocks = pattern_rows.reshape(block_count // 4, 4, NSEL)
    own_blocks = jnp.arange(block_count, dtype=jnp.int32).reshape(block_count // 4, 4)
    scaling = 1.0 / math.sqrt(head_dim)
    causal = jnp.arange(BLOCK)[:, None] >= jnp.arange(BLOCK)[None, :]

    def one_group(operands):
        q_group, chosen_group, own_group = operands
        is_live = chosen_group >= 0
        clamped = jnp.maximum(chosen_group, 0).astype(jnp.int32)
        key_sel = key_blocks[clamped]
        value_sel = value_blocks[clamped]
        scores = jnp.einsum('qthd,qskd->qhtsk', q_group.astype(jnp.float32), key_sel.astype(jnp.float32)) * scaling
        on_diagonal = clamped == own_group[:, None]
        allowed = is_live[:, None, None, :, None] & (jnp.logical_not(on_diagonal)[:, None, None, :, None] | causal[None, None, :, None, :])
        scores = jnp.where(allowed, scores, -1e+30)
        row_max = lax.optimization_barrier(jnp.max(scores, axis=(3, 4), keepdims=True))
        weights = jnp.exp(scores - row_max)
        row_total = lax.optimization_barrier(jnp.sum(weights, axis=(3, 4), keepdims=True))
        probability = (weights / row_total).astype(jnp.bfloat16)
        mixed_rows = jnp.einsum('qhtsk,qskd->qthd', probability.astype(jnp.float32), value_sel.astype(jnp.float32))
        return mixed_rows.astype(jnp.bfloat16)
    gathered_out = lax.map(one_group, (query_blocks, chosen_blocks, own_blocks))
    return gathered_out.reshape(token_count, head_count * head_dim)

def reference(residual, query_rows, key_rows, value_rows, pattern):
    group_size = HQ // HK
    results = []
    for section in range(SEGMENTS):
        previous = (section - 1) % SEGMENTS
        running = residual[previous].astype(jnp.float32)
        layer_total = jnp.zeros((TOKENS, HQ * HD), jnp.float32)
        for layer_no in range(LAYERS):
            q_heads = jnp.moveaxis(query_rows[section, layer_no].reshape(TOKENS, HK, group_size, HD), 1, 0)
            k_heads = jnp.moveaxis(key_rows[section, layer_no].reshape(TOKENS, HK, HD), 1, 0)
            v_heads = jnp.moveaxis(value_rows[section, layer_no].reshape(TOKENS, HK, HD), 1, 0)

            def per_head(operands):
                return attend(operands[0], operands[1], operands[2], operands[3])
            attended = lax.map(per_head, (q_heads, k_heads, v_heads, pattern[section, layer_no]))
            attended = jnp.moveaxis(attended, 0, 1).reshape(TOKENS, HQ * HD)
            layer_total = layer_total + attended.astype(jnp.float32)
        layer_sum = layer_total.astype(jnp.bfloat16)
        results.append(running + layer_sum.astype(jnp.float32))
    return jnp.stack(results)
```

```python
import functools
import math

import jax
import jax.numpy as jnp
from jax import lax
from jax.experimental import pallas as pl
from jax.experimental.pallas import tpu as pltpu
from jax.sharding import PartitionSpec as P

HQ = 64
HK = 8
HD = 128
CHUNKS = (2, 2, 2, 2)


def columns_of(ring):
    width = 1
    while 2 * (2 * width) ** 2 <= ring:
        width *= 2
    return width


def rotated(array, axis, move):
    size = lax.axis_size(axis)
    return lax.ppermute(array, axis, [(i, move(i)) for i in range(size)])


def collected(block, width):
    ring = lax.axis_size("seq")
    up = lambda i: (i + width) % ring
    found = []
    held = block
    for step in range(ring // width):
        if step:
            held = rotated(held, "seq", up)
        found.append(held)
        for by in range(1, width):
            across = lambda i, by=by: i // width * width + (i + by) % width
            found.append(rotated(held, "seq", across))
    return found


def attend_body(layers, first_head, live_ref, q_ref, *refs):
    kv_refs, (carried_ref, _, out_ref) = refs[:-3], refs[-3:]
    tokens = q_ref.shape[1]
    group = pl.program_id(0)
    factor = math.log2(math.e) / math.sqrt(HD)
    row = lax.broadcasted_iota(jnp.int32, (tokens, tokens), 0)
    col = lax.broadcasted_iota(jnp.int32, (tokens, tokens), 1)
    causal = row >= col
    ones = jnp.ones((tokens, HD), jnp.bfloat16)
    for layer in range(layers):
        own = kv_refs[0]
        visible_key = jnp.broadcast_to(own[layer, 0:1, :], (tokens, HD))
        keys, values, weights = [own[layer]], [own[layers + layer]], [ones]
        for place in range(1, len(kv_refs)):
            live = live_ref[layer, first_head + group, place] > 0
            keys.append(jnp.where(live, kv_refs[place][layer], visible_key))
            values.append(jnp.where(live, kv_refs[place][layers + layer], jnp.zeros_like(ones)))
            weights.append(jnp.where(live, ones, jnp.zeros_like(ones)))
        keys = jnp.concatenate(keys, axis=0)
        values = jnp.concatenate(
            [jnp.concatenate(values, axis=0), jnp.concatenate(weights, axis=0)], axis=1
        )
        for head in range(q_ref.shape[2] // HD):
            lanes = slice(head * HD, (head + 1) * HD)
            scores = lax.dot_general(
                q_ref[layer, :, lanes],
                keys,
                (((1,), (1,)), ((), ())),
                preferred_element_type=jnp.float32,
            )
            own_scores = jnp.where(causal, scores[:, :tokens], -1e30)
            scores = jnp.concatenate([own_scores, scores[:, tokens:]], axis=1)
            row_max = jnp.max(scores, axis=1, keepdims=True)
            weight = jnp.exp2((scores - row_max) * factor).astype(jnp.bfloat16)
            mixed = jnp.dot(weight, values, preferred_element_type=jnp.float32)
            attended = mixed[:, :HD] / mixed[:, HD:]
            total = attended.astype(jnp.bfloat16).astype(jnp.float32)
            if layer:
                total = out_ref[:, lanes] + total
            if layer == layers - 1:
                total = total.astype(jnp.bfloat16).astype(jnp.float32)
                total = carried_ref[:, lanes].astype(jnp.float32) + total
            out_ref[:, lanes] = total


def attend(live, queries, blocks, carried, out, first_head):
    layers, tokens, width = queries.shape
    heads = blocks[0].shape[2] // HD
    lanes = width // HK
    operands = [live, queries, *blocks, carried]
    whole = pl.BlockSpec(memory_space=pl.ANY)
    aliases = {}
    if out is None:
        out = carried
    else:
        aliases = {len(operands): 0}
    return pl.pallas_call(
        functools.partial(attend_body, layers, first_head),
        grid_spec=pltpu.PrefetchScalarGridSpec(
            num_scalar_prefetch=1,
            grid=(heads,),
            in_specs=[
                pl.BlockSpec((layers, tokens, lanes), lambda g, _: (0, 0, first_head + g)),
                *[pl.BlockSpec((2 * layers, tokens, HD), lambda g, _: (0, 0, g)) for _ in blocks],
                pl.BlockSpec((tokens, lanes), lambda g, _: (0, first_head + g)),
                whole,
            ],
            out_specs=pl.BlockSpec((tokens, lanes), lambda g, _: (0, first_head + g)),
        ),
        out_shape=jax.ShapeDtypeStruct((tokens, width), jnp.float32),
        input_output_aliases=aliases,
        compiler_params=pltpu.CompilerParams(vmem_limit_bytes=32 << 20),
        cost_estimate=pl.CostEstimate(
            flops=4 * layers * tokens * lanes * heads * tokens * len(blocks),
            bytes_accessed=heads * tokens * (layers * lanes * 2 + lanes * 6),
            transcendentals=layers * tokens * (lanes // HD) * heads * tokens * len(blocks),
        ),
    )(*operands, out)


def local(residual, query_rows, key_rows, value_rows, pattern):
    ring = lax.axis_size("seq")
    segments = lax.axis_size("segment")
    width = columns_of(ring)
    me = lax.axis_index("seq")
    carried = rotated(residual[0], "segment", lambda i: (i + 1) % segments)
    place = jnp.arange(ring, dtype=jnp.int32)
    rows_below, shift = place // width, place % width
    held_block = (me // width - rows_below) % (ring // width) * width + (me - shift) % width
    chosen = lax.dynamic_index_in_dim(pattern[0], me, axis=2, keepdims=False)
    live = jnp.any(chosen[:, :, :, None] == held_block, axis=2).astype(jnp.int32)
    out = None
    first_head = 0
    for heads in CHUNKS:
        lanes = slice(first_head * HD, (first_head + heads) * HD)
        block = jnp.concatenate([key_rows[0, :, :, lanes], value_rows[0, :, :, lanes]], axis=0)
        out = attend(live, query_rows[0], collected(block, width), carried, out, first_head)
        first_head += heads
    return out[None]


def solution(mesh):
    return jax.shard_map(
        local,
        mesh=mesh,
        in_specs=(
            P("segment", "seq", None),
            P("segment", None, "seq", None),
            P("segment", None, "seq", None),
            P("segment", None, "seq", None),
            P("segment", None, None, None, None),
        ),
        out_specs=P("segment", "seq", None),
        check_vma=False,
    )
```

```python
import functools
import math

import jax
import jax.numpy as jnp
from jax import lax
from jax.experimental import pallas as pl
from jax.experimental.pallas import tpu as pltpu
from jax.sharding import PartitionSpec as P

HQ = 64
HK = 8
HD = 128
AHEAD = 4
NO_COST = pl.CostEstimate(flops=0, bytes_accessed=0, transcendentals=0)


def columns_of(ring):
    width = 1
    while 2 * (2 * width) ** 2 <= ring:
        width *= 2
    return width


def rotated(array, axis, move):
    size = lax.axis_size(axis)
    return lax.ppermute(array, axis, [(i, move(i)) for i in range(size)])


def tied(array, others):
    if not others:
        return array
    anywhere = pl.BlockSpec(memory_space=pl.ANY)
    return pl.pallas_call(
        lambda *_: None,
        in_specs=[anywhere] * (1 + len(others)),
        out_specs=anywhere,
        out_shape=jax.ShapeDtypeStruct(array.shape, array.dtype),
        input_output_aliases={0: 0},
        cost_estimate=NO_COST,
    )(array, *others)


def attend_body(stage, layers, first_head, places, live_ref, q_ref, *refs):
    operands = 1 + max(operand for _, operand, _ in places)
    kv_refs, refs = refs[:operands], refs[operands:]
    resumes, ends = stage in ("next", "last"), stage in ("whole", "last")
    refs = list(refs)
    carried_ref = refs.pop(0) if ends else None
    before_ref = refs.pop(0) if resumes else None
    if ends:
        _, out_ref = refs
    else:
        (sums_ref,) = refs
    tokens = q_ref.shape[1]
    group = pl.program_id(0)
    factor = math.log2(math.e) / math.sqrt(HD)
    row = lax.broadcasted_iota(jnp.int32, (tokens, tokens), 0)
    col = lax.broadcasted_iota(jnp.int32, (tokens, tokens), 1)
    causal = row >= col
    ones = jnp.ones((tokens, HD), jnp.bfloat16)
    heads = q_ref.shape[2] // HD
    for layer in range(layers):
        visible_key = jnp.broadcast_to(kv_refs[0][layer, 0:1, :], (tokens, HD))
        keys, values, weights = [], [], []
        for place, operand, base in places:
            key = kv_refs[operand][base + layer]
            value = kv_refs[operand][base + layers + layer]
            if place:
                live = live_ref[layer, first_head + group, place] > 0
                keys.append(jnp.where(live, key, visible_key))
                values.append(jnp.where(live, value, jnp.zeros_like(value)))
                weights.append(jnp.where(live, ones, jnp.zeros_like(ones)))
            elif not resumes:
                keys.append(key)
                values.append(value)
                weights.append(ones)
        keys = jnp.concatenate(keys, axis=0)
        values = jnp.concatenate(
            [jnp.concatenate(values, axis=0), jnp.concatenate(weights, axis=0)], axis=1
        )
        for head in range(heads):
            lanes = slice(head * HD, (head + 1) * HD)
            scores = lax.dot_general(
                q_ref[layer, :, lanes],
                keys,
                (((1,), (1,)), ((), ())),
                preferred_element_type=jnp.float32,
            )
            if not resumes:
                own_scores = jnp.where(causal, scores[:, :tokens], -1e30)
                scores = jnp.concatenate([own_scores, scores[:, tokens:]], axis=1)
            row_max = jnp.max(scores, axis=1, keepdims=True)
            if resumes:
                max_before = before_ref[1, layer, :, lanes]
                row_max = jnp.maximum(row_max, max_before)
                shrink = jnp.exp2((max_before - row_max) * factor)
                scores = scores - jnp.concatenate([row_max] * (scores.shape[1] // HD), axis=1)
            else:
                scores = scores - row_max
            weight = jnp.exp2(scores * factor).astype(jnp.bfloat16)
            mixed = jnp.dot(weight, values, preferred_element_type=jnp.float32)
            mixed, total = mixed[:, :HD], mixed[:, HD:]
            if resumes:
                mixed = before_ref[0, layer, :, lanes] * shrink + mixed
                total = shrink + total
            if not ends:
                sums_ref[0, layer, :, lanes] = mixed / total
                sums_ref[1, layer, :, lanes] = row_max + jnp.log2(total) / factor
                continue
            attended = (mixed / total).astype(jnp.bfloat16).astype(jnp.float32)
            if layer:
                attended = out_ref[:, lanes] + attended
            if layer == layers - 1:
                attended = attended.astype(jnp.bfloat16).astype(jnp.float32)
                attended = carried_ref[:, lanes].astype(jnp.float32) + attended
            out_ref[:, lanes] = attended


def attend(stage, live, queries, blocks, carried, before, out, first_head, heads):
    layers, tokens, width = queries.shape
    lanes = width // HK
    anywhere = pl.BlockSpec(memory_space=pl.ANY)
    columns = pl.BlockSpec((tokens, lanes), lambda g, _: (0, first_head + g))
    sums = pl.BlockSpec((2, layers, tokens, lanes), lambda g, _: (0, 0, 0, g))
    arrays, places = [], []
    for place, (array, base) in blocks.items():
        if not any(array is other for other in arrays):
            arrays.append(array)
        places.append((place, [array is other for other in arrays].index(True), base))
    operands = [live, queries, *arrays]
    in_specs = [
        pl.BlockSpec((layers, tokens, lanes), lambda g, _: (0, 0, first_head + g)),
        *[pl.BlockSpec((a.shape[0], tokens, HD), lambda g, _: (0, 0, g)) for a in arrays],
    ]
    aliases = {}
    ends = stage in ("whole", "last")
    if ends:
        operands.append(carried)
        in_specs.append(columns)
    if before is not None:
        operands.append(before)
        in_specs.append(sums)
    if ends:
        if out is not None:
            aliases = {len(operands): 0}
        operands.append(carried if out is None else out)
        in_specs.append(anywhere)
        out_specs = columns
        out_shape = jax.ShapeDtypeStruct((tokens, width), jnp.float32)
    else:
        out_specs = sums
        out_shape = jax.ShapeDtypeStruct((2, layers, tokens, lanes * heads), jnp.float32)
    return pl.pallas_call(
        functools.partial(attend_body, stage, layers, first_head, tuple(places)),
        grid_spec=pltpu.PrefetchScalarGridSpec(
            num_scalar_prefetch=1, grid=(heads,), in_specs=in_specs, out_specs=out_specs
        ),
        out_shape=out_shape,
        input_output_aliases=aliases,
        compiler_params=pltpu.CompilerParams(vmem_limit_bytes=60 << 20),
        cost_estimate=NO_COST,
    )(*operands)


class Stream:
    def __init__(self, block, ring, width):
        self.rows, self.width = ring // width, width
        self.up = lambda i: (i + width) % ring
        self.held, self.across, self.blocks = block, [], {}

    def go(self, step, others=()):
        here = tied(self.held, [*self.across, *others])
        width = self.width
        if step < self.rows - 1:
            self.held = rotated(here, "seq", self.up)
        self.across = [
            rotated(here, "seq", lambda i, by=by: i // width * width + (i + by) % width)
            for by in range(1, width)
        ]
        for by, block in enumerate([here, *self.across]):
            self.blocks[step * width + by] = block, 0


def local(residual, query_rows, key_rows, value_rows, pattern):
    ring = lax.axis_size("seq")
    segments = lax.axis_size("segment")
    width = columns_of(ring)
    rows = ring // width
    me = lax.axis_index("seq")
    carried = rotated(residual[0], "segment", lambda i: (i + 1) % segments)
    place = jnp.arange(ring, dtype=jnp.int32)
    rows_below, shift = place // width, place % width
    held_block = (me // width - rows_below) % rows * width + (me - shift) % width
    chosen = lax.dynamic_index_in_dim(pattern[0], me, axis=2, keepdims=False)
    live = jnp.any(chosen[:, :, :, None] == held_block, axis=2).astype(jnp.int32)

    def stream(first_head, heads):
        lanes = slice(first_head * HD, (first_head + heads) * HD)
        block = jnp.concatenate([key_rows[0, :, :, lanes], value_rows[0, :, :, lanes]], axis=0)
        return Stream(block, ring, width)

    attend_here = functools.partial(attend, live=live, queries=query_rows[0], carried=carried)
    firsts, sizes = (0, AHEAD), (AHEAD, HK - AHEAD)
    streams = [stream(first, size) for first, size in zip(firsts, sizes, strict=True)]
    cut = rows // 2

    def attended(stage, which, steps, state=None, out=None):
        blocks = streams[which].blocks
        blocks = {k: v for k, v in blocks.items() if k // width in steps or (k == 0 and state is not None)}
        return attend_here(
            stage, blocks=blocks, before=state, out=out, first_head=firsts[which], heads=sizes[which]
        )

    states = [None, None]
    for step in range(rows):
        streams[0].go(step, [states[1]] if step == rows - 1 else [])
        if step + 1 == cut:
            states[0] = attended("first", 0, range(cut))
        streams[1].go(step, [states[0]] if step == rows - 2 else [])
        if step + 1 == cut:
            states[1] = attended("first", 1, range(cut))
    out = attended("last", 0, range(cut, rows), states[0])
    out = attended("last", 1, range(cut, rows), states[1], out)
    return out[None]


def solution(mesh):
    return jax.shard_map(
        local,
        mesh=mesh,
        in_specs=(
            P("segment", "seq", None),
            P("segment", None, "seq", None),
            P("segment", None, "seq", None),
            P("segment", None, "seq", None),
            P("segment", None, None, None, None),
        ),
        out_specs=P("segment", "seq", None),
        check_vma=False,
    )
```

```python
import functools
import math

import jax
import jax.numpy as jnp
from jax import lax
from jax.experimental import pallas as pl
from jax.experimental.pallas import tpu as pltpu
from jax.sharding import PartitionSpec as P

HQ = 64
HK = 8
HD = 128
AHEAD = 4
NO_COST = pl.CostEstimate(flops=0, bytes_accessed=0, transcendentals=0)


def columns_of(ring):
    width = 1
    while 2 * (2 * width) ** 2 <= ring:
        width *= 2
    return width


def rotated(array, axis, move):
    size = lax.axis_size(axis)
    return lax.ppermute(array, axis, [(i, move(i)) for i in range(size)])


def tied(array, others):
    if not others:
        return array
    anywhere = pl.BlockSpec(memory_space=pl.ANY)
    return pl.pallas_call(
        lambda *_: None,
        in_specs=[anywhere] * (1 + len(others)),
        out_specs=anywhere,
        out_shape=jax.ShapeDtypeStruct(array.shape, array.dtype),
        input_output_aliases={0: 0},
        cost_estimate=NO_COST,
    )(array, *others)


def attend_body(stage, layers, first_head, places, live_ref, q_ref, *refs):
    operands = 1 + max(operand for _, operand, _ in places)
    kv_refs, refs = refs[:operands], refs[operands:]
    resumes, ends = stage in ("next", "last"), stage in ("whole", "last")
    refs = list(refs)
    carried_ref = refs.pop(0) if ends else None
    means_before, logs_before = (refs.pop(0), refs.pop(0)) if resumes else (None, None)
    if ends:
        _, out_ref = refs
    else:
        means_ref, logs_ref = refs
    tokens = q_ref.shape[1]
    group = pl.program_id(0)
    factor = math.log2(math.e) / math.sqrt(HD)
    row = lax.broadcasted_iota(jnp.int32, (tokens, tokens), 0)
    col = lax.broadcasted_iota(jnp.int32, (tokens, tokens), 1)
    causal = row >= col
    ones = jnp.ones((tokens, HD), jnp.bfloat16)
    heads = q_ref.shape[2] // HD
    for layer in range(layers):
        visible_key = jnp.broadcast_to(kv_refs[0][layer, 0:1, :], (tokens, HD))
        keys, values, weights = [], [], []
        for place, operand, base in places:
            key = kv_refs[operand][base + layer]
            value = kv_refs[operand][base + layers + layer]
            if place:
                live = live_ref[layer, first_head + group, place] > 0
                keys.append(jnp.where(live, key, visible_key))
                values.append(jnp.where(live, value, jnp.zeros_like(value)))
                weights.append(jnp.where(live, ones, jnp.zeros_like(ones)))
            elif not resumes:
                keys.append(key)
                values.append(value)
                weights.append(ones)
        keys = jnp.concatenate(keys, axis=0)
        values = jnp.concatenate(
            [jnp.concatenate(values, axis=0), jnp.concatenate(weights, axis=0)], axis=1
        )
        for head in range(heads):
            lanes = slice(head * HD, (head + 1) * HD)
            scores = lax.dot_general(
                q_ref[layer, :, lanes],
                keys,
                (((1,), (1,)), ((), ())),
                preferred_element_type=jnp.float32,
            )
            if not resumes:
                own_scores = jnp.where(causal, scores[:, :tokens], -1e30)
                scores = jnp.concatenate([own_scores, scores[:, tokens:]], axis=1)
            row_max = jnp.max(scores, axis=1, keepdims=True)
            if resumes:
                max_before = logs_before[layer, :, lanes]
                row_max = jnp.maximum(row_max, max_before)
                shrink = jnp.exp2((max_before - row_max) * factor)
                scores = scores - jnp.concatenate([row_max] * (scores.shape[1] // HD), axis=1)
            else:
                scores = scores - row_max
            weight = jnp.exp2(scores * factor).astype(jnp.bfloat16)
            mixed = jnp.dot(weight, values, preferred_element_type=jnp.float32)
            mixed, total = mixed[:, :HD], mixed[:, HD:]
            if resumes:
                mixed = means_before[layer, :, lanes].astype(jnp.float32) * shrink + mixed
                total = shrink + total
            if not ends:
                means_ref[layer, :, lanes] = (mixed / total).astype(means_ref.dtype)
                logs_ref[layer, :, lanes] = row_max + jnp.log2(total) * (1.0 / factor)
                continue
            attended = (mixed / total).astype(jnp.bfloat16).astype(jnp.float32)
            if layer:
                attended = out_ref[:, lanes] + attended
            if layer == layers - 1:
                attended = attended.astype(jnp.bfloat16).astype(jnp.float32)
                attended = carried_ref[:, lanes].astype(jnp.float32) + attended
            out_ref[:, lanes] = attended


def attend(stage, live, queries, blocks, carried, before, out, first_head, heads):
    layers, tokens, width = queries.shape
    lanes = width // HK
    anywhere = pl.BlockSpec(memory_space=pl.ANY)
    columns = pl.BlockSpec((tokens, lanes), lambda g, _: (0, first_head + g))
    state = pl.BlockSpec((layers, tokens, lanes), lambda g, _: (0, 0, g))
    arrays, places = [], []
    for place, (array, base) in blocks.items():
        if not any(array is other for other in arrays):
            arrays.append(array)
        places.append((place, [array is other for other in arrays].index(True), base))
    operands = [live, queries, *arrays]
    in_specs = [
        pl.BlockSpec((layers, tokens, lanes), lambda g, _: (0, 0, first_head + g)),
        *[pl.BlockSpec((a.shape[0], tokens, HD), lambda g, _: (0, 0, g)) for a in arrays],
    ]
    aliases = {}
    ends = stage in ("whole", "last")
    if ends:
        operands.append(carried)
        in_specs.append(columns)
    if before is not None:
        operands += before
        in_specs += [state] * 2
    if ends:
        if out is not None:
            aliases = {len(operands): 0}
        operands.append(carried if out is None else out)
        in_specs.append(anywhere)
        out_specs = columns
        out_shape = jax.ShapeDtypeStruct((tokens, width), jnp.float32)
    else:
        out_specs = [state] * 2
        out_shape = [
            jax.ShapeDtypeStruct((layers, tokens, lanes * heads), dtype)
            for dtype in (jnp.bfloat16, jnp.float32)
        ]
    return pl.pallas_call(
        functools.partial(attend_body, stage, layers, first_head, tuple(places)),
        grid_spec=pltpu.PrefetchScalarGridSpec(
            num_scalar_prefetch=1, grid=(heads,), in_specs=in_specs, out_specs=out_specs
        ),
        out_shape=out_shape,
        input_output_aliases=aliases,
        compiler_params=pltpu.CompilerParams(vmem_limit_bytes=60 << 20),
        cost_estimate=NO_COST,
    )(*operands)


class Stream:
    def __init__(self, block, ring, width):
        self.rows, self.width = ring // width, width
        self.up = lambda i: (i + width) % ring
        self.held, self.across, self.blocks = block, [], {}

    def go(self, step, others=()):
        here = tied(self.held, [*self.across, *others])
        width = self.width
        if step < self.rows - 1:
            self.held = rotated(here, "seq", self.up)
        self.across = [
            rotated(here, "seq", lambda i, by=by: i // width * width + (i + by) % width)
            for by in range(1, width)
        ]
        for by, block in enumerate([here, *self.across]):
            self.blocks[step * width + by] = block, 0


def local(residual, query_rows, key_rows, value_rows, pattern):
    ring = lax.axis_size("seq")
    segments = lax.axis_size("segment")
    width = columns_of(ring)
    rows = ring // width
    me = lax.axis_index("seq")
    carried = rotated(residual[0], "segment", lambda i: (i + 1) % segments)
    place = jnp.arange(ring, dtype=jnp.int32)
    rows_below, shift = place // width, place % width
    held_block = (me // width - rows_below) % rows * width + (me - shift) % width
    chosen = lax.dynamic_index_in_dim(pattern[0], me, axis=2, keepdims=False)
    live = jnp.any(chosen[:, :, :, None] == held_block, axis=2).astype(jnp.int32)

    def stream(first_head, heads):
        lanes = slice(first_head * HD, (first_head + heads) * HD)
        block = jnp.concatenate([key_rows[0, :, :, lanes], value_rows[0, :, :, lanes]], axis=0)
        return Stream(block, ring, width)

    attend_here = functools.partial(attend, live=live, queries=query_rows[0], carried=carried)
    firsts, sizes = (0, AHEAD), (AHEAD, HK - AHEAD)
    streams = [stream(first, size) for first, size in zip(firsts, sizes, strict=True)]
    cut = rows // 2

    def attended(stage, which, steps, state=None, out=None):
        blocks = streams[which].blocks
        blocks = {k: v for k, v in blocks.items() if k // width in steps or (k == 0 and state is not None)}
        return attend_here(
            stage, blocks=blocks, before=state, out=out, first_head=firsts[which], heads=sizes[which]
        )

    states = [None, None]
    for step in range(rows):
        streams[0].go(step, states[1] if step == rows - 1 else [])
        if step + 1 == cut:
            states[0] = attended("first", 0, range(cut))
        if step == rows - 1:
            states[0] = attended("next", 0, range(cut, rows - 1), states[0])
        streams[1].go(step, states[0] if step >= rows - 2 else [])
        if step + 1 == cut:
            states[1] = attended("first", 1, range(cut))
    out = attended("last", 0, range(rows - 1, rows), states[0])
    out = attended("last", 1, range(cut, rows), states[1], out)
    return out[None]


def solution(mesh):
    return jax.shard_map(
        local,
        mesh=mesh,
        in_specs=(
            P("segment", "seq", None),
            P("segment", None, "seq", None),
            P("segment", None, "seq", None),
            P("segment", None, "seq", None),
            P("segment", None, None, None, None),
        ),
        out_specs=P("segment", "seq", None),
        check_vma=False,
    )
```
